32 devices in a mesh: grp: 2 (over y), seq: 8 (over z, x), doc: 2 (over core).
Axes of the slice: x: 2, y: 2, z: 4, core: 2. Of those that a mesh axis runs over, the one named last changes fastest.
Arguments:
- state: bfloat16 [32, 3, 1024, 1024], P(('grp', 'seq', 'doc')), parts along dimension 0, may hold values from -0.1875 to 0.1875
- keys: bfloat16 [2, 32, 384, 1024], P(None, ('grp', 'seq', 'doc')), parts along dimension 1, may hold values from -6 to 6
- values: bfloat16 [2, 32, 384, 1024], P(None, ('grp', 'seq', 'doc')), parts along dimension 1, may hold values from -6 to 6
- queries: bfloat16 [2, 32, 384, 1024], P(None, ('grp', 'seq', 'doc')), parts along dimension 1, may hold values from -6 to 6
- rates: float32 [2, 32, 384], P(None, 'grp'), parts along dimension 1, may hold values from 0.001 to 0.01
- remaining: int32 [32], P('grp'), parts along dimension 0, may hold values from 1 to 2
- first_owner: int32 [32], P('grp'), parts along dimension 0, may hold values from 0 to 15, each once
- migration: int32 [32], P('grp'), parts along dimension 0, may hold values from 0 to 15, as said below
Outputs:
- round_one: bfloat16 [32, 384, 1024], P(('grp', 'seq', 'doc')), parts along dimension 0
- round_two: bfloat16 [32, 384, 1024], P(('grp', 'seq', 'doc')), parts along dimension 0
The draws below stay inside these ranges and needn't reach their ends.
There are 2 independent parts, one for each index of `grp`. The reference program is written for one: setup_inputs(seed, part) draws one part's arguments, and reference() takes and returns one part's arrays. A program takes and returns all parts, laid end to end along the dimension named above; each array names one. Nothing has to cross between parts.
Inputs may be any that keep to these rules, and one draw needn't show every extreme that they name: first_owner is a permutation: document d starts with the fast weights state[first_owner[d]]. migration is a permutation that leaves all but exactly 4 owners in place. `remaining`: a document has a round-two block exactly where its entry is 2.
All inputs are finite; a program needn't handle non-finite values.
Results may differ from the reference program's by a relative error of at most 0.012.
Values may be sent and summed in bfloat16 or wider, within the bound.
No kernel may reach another device: no remote copies, remote signals or barrier semaphores. Data moves between devices by JAX's collectives and lax.ppermute only.
A program may use at most 128 MiB of HBM per device.

```python
import math
import jax
import jax.numpy as jnp
from jax import lax

D = 1024
CH = 384
ROUNDS = 2
DOCS = 16
OWNERS = 16


def draw_migration(key, part):
    shuffled = jax.random.permutation(key, OWNERS).astype(jnp.int32)
    moving = OWNERS // 4
    chosen = shuffled[:moving]
    target = jnp.roll(chosen, 1)
    initial = jnp.arange(OWNERS, dtype=jnp.int32)
    return initial.at[chosen].set(target).astype(jnp.int32)


def plant(entries, rng, low, top_value):
    dims = entries.shape
    index_at = [jax.random.randint(jax.random.fold_in(rng, axis), (), 0, dims[axis]) for axis in range(len(dims))]
    entries = entries.at[tuple(index_at)].set(low)
    longest = dims.index(max(dims))
    index_at[longest] = (index_at[longest] + 1) % dims[longest]
    return entries.at[tuple(index_at)].set(top_value)


def steps_of(own_key, extent, split, low, top_value):
    level, own = 1.0, jax.random.fold_in(own_key, 6)
    for dim, blocks in split:
        steps = jnp.exp(jax.random.uniform(jax.random.fold_in(own, dim), (blocks,), jnp.float32, low / len(split), top_value / len(split)))
        level = level * jnp.repeat(steps, extent[dim] // blocks).reshape([-1 if axis == dim else 1 for axis in range(len(extent))])
    return level


def centred(stream_key, shape, width, bound, split=(), kind=jnp.bfloat16):
    result = width * jax.random.normal(stream_key, shape, jnp.float32)
    if split:
        result = result * steps_of(stream_key, shape, split, -0.22, 0.18)
    return jnp.clip(result, -bound, bound).astype(kind)


def setup_inputs(seed: int = 0, part: int = 0) -> dict:
    arg_keys = jax.random.split(jax.random.key(seed), 9)
    own_keys = jax.random.split(jax.random.fold_in(arg_keys[8], part), 9)
    state = centred(own_keys[0], (OWNERS, 3, D, D), D ** -0.5, 0.1875, ((0, 16),))
    keys = centred(own_keys[1], (ROUNDS, DOCS, CH, D), 1.0, 6.0, ((1, 16),))
    values = centred(own_keys[2], (ROUNDS, DOCS, CH, D), 1.0, 6.0, ((1, 16),))
    queries = centred(own_keys[3], (ROUNDS, DOCS, CH, D), 1.0, 6.0, ((1, 16),))
    rates = jnp.clip(jnp.exp(jax.random.uniform(own_keys[4], (ROUNDS, DOCS, CH), jnp.float32, math.log(0.001), math.log(0.01))), 0.001, 0.01)
    remaining = plant(jax.random.randint(own_keys[5], (DOCS,), 1, 3), jax.random.fold_in(own_keys[5], 1), 1, 2).astype(jnp.int32)
    first_owner = jax.random.permutation(own_keys[6], DOCS).astype(jnp.int32)
    migration = draw_migration(jax.random.fold_in(jax.random.fold_in(arg_keys[8], part), 71), part)
    return {"state": state, "keys": keys, "values": values, "queries": queries, "rates": rates, "remaining": remaining, "first_owner": first_owner, "migration": migration}


EPSILON = 1e-06

def swiglu_apply(weights, inputs):
    gate_pre = jnp.dot(inputs, weights[0], preferred_element_type=jnp.float32)
    upward = jnp.dot(inputs, weights[1], preferred_element_type=jnp.float32)
    hidden = (jax.nn.silu(gate_pre) * upward).astype(jnp.bfloat16)
    return jnp.dot(hidden, weights[2], preferred_element_type=jnp.float32)

def renorm(weight, gradient):
    before = weight.astype(jnp.float32)
    stepped = before - gradient
    factor = jnp.sqrt(lax.optimization_barrier(jnp.mean(before * before, axis=0)) + EPSILON) / jnp.sqrt(lax.optimization_barrier(jnp.mean(stepped * stepped, axis=0)) + EPSILON)
    return (stepped * factor[None, :]).astype(jnp.bfloat16)

def fast_update(weights, keys_rows, values_rows, rate_rows):
    gate_pre = jnp.dot(keys_rows, weights[0], preferred_element_type=jnp.float32)
    upward = jnp.dot(keys_rows, weights[1], preferred_element_type=jnp.float32)
    sigmoid_gate = jax.nn.sigmoid(gate_pre)
    active = gate_pre * sigmoid_gate
    hidden = (active * upward).astype(jnp.bfloat16)
    scaled_values = (rate_rows[:, None] * values_rows.astype(jnp.float32)).astype(jnp.bfloat16)
    grad_down = -jnp.dot(hidden.T, scaled_values, preferred_element_type=jnp.float32)
    grad_hidden = -jnp.dot(scaled_values, weights[2].T, preferred_element_type=jnp.float32)
    slope = sigmoid_gate * (1.0 + gate_pre * (1.0 - sigmoid_gate))
    grad_gate = (grad_hidden * upward * slope).astype(jnp.bfloat16)
    grad_up = (grad_hidden * active).astype(jnp.bfloat16)
    grad_first = jnp.dot(keys_rows.T, grad_gate, preferred_element_type=jnp.float32)
    grad_third = jnp.dot(keys_rows.T, grad_up, preferred_element_type=jnp.float32)
    return jnp.stack([renorm(weights[0], grad_first), renorm(weights[1], grad_third), renorm(weights[2], grad_down)])

def inverse_of(permuted):
    count = permuted.shape[0]
    labels = jnp.arange(count, dtype=jnp.int32)
    return lax.optimization_barrier(jnp.sum(jnp.where(permuted[None, :] == labels[:, None], labels[None, :], 0), axis=1)).astype(jnp.int32)

def reference(state, keys, values, queries, rates, remaining, first_owner, migration):
    doc_ids = jnp.arange(DOCS, dtype=jnp.int32)

    def one_doc(doc_index):
        owner_now = first_owner[doc_index]
        first_state = fast_update(state[owner_now], keys[0, doc_index], values[0, doc_index], rates[0, doc_index])
        out_first = swiglu_apply(first_state, queries[0, doc_index]).astype(jnp.bfloat16)
        second_state = fast_update(first_state, keys[1, doc_index], values[1, doc_index], rates[1, doc_index])
        out_second = swiglu_apply(second_state, queries[1, doc_index])
        is_live = remaining[doc_index] >= 2
        out_second = jnp.where(is_live, out_second, jnp.float32(0.0)).astype(jnp.bfloat16)
        return (out_first, out_second)
    round_one, by_doc = lax.map(one_doc, doc_ids)
    doc_second = inverse_of(migration[first_owner])
    round_two = jnp.take(by_doc, doc_second, axis=0)
    return (round_one, round_two)
```

```python
import functools

import jax
import jax.numpy as jnp
from jax import lax
from jax.experimental import pallas as pl
from jax.experimental.pallas import tpu as pltpu
from jax.sharding import Mesh, PartitionSpec as P

EPSILON = 1e-06
LEVEL = ("x", "core")
GROUP = ("z", "x", "core")
EXTRA = 2


def swiglu_apply(weights, inputs):
    gate_pre = jnp.dot(inputs, weights[0], preferred_element_type=jnp.float32)
    upward = jnp.dot(inputs, weights[1], preferred_element_type=jnp.float32)
    hidden = (jax.nn.silu(gate_pre) * upward).astype(jnp.bfloat16)
    return jnp.dot(hidden, weights[2], preferred_element_type=jnp.float32)


def renorm(weight, gradient):
    before = weight.astype(jnp.float32)
    stepped = before - gradient
    factor = jnp.sqrt(jnp.mean(before * before, axis=0) + EPSILON) / jnp.sqrt(
        jnp.mean(stepped * stepped, axis=0) + EPSILON
    )
    return (stepped * factor[None, :]).astype(jnp.bfloat16)


def fast_update(weights, keys_rows, values_rows, rate_rows):
    gate_pre = jnp.dot(keys_rows, weights[0], preferred_element_type=jnp.float32)
    upward = jnp.dot(keys_rows, weights[1], preferred_element_type=jnp.float32)
    sigmoid_gate = jax.nn.sigmoid(gate_pre)
    active = gate_pre * sigmoid_gate
    hidden = (active * upward).astype(jnp.bfloat16)
    scaled_values = (rate_rows[:, None] * values_rows.astype(jnp.float32)).astype(jnp.bfloat16)
    grad_down = -jnp.dot(hidden.T, scaled_values, preferred_element_type=jnp.float32)
    grad_hidden = -jnp.dot(scaled_values, weights[2].T, preferred_element_type=jnp.float32)
    slope = sigmoid_gate * (1.0 + gate_pre * (1.0 - sigmoid_gate))
    grad_gate = (grad_hidden * upward * slope).astype(jnp.bfloat16)
    grad_up = (grad_hidden * active).astype(jnp.bfloat16)
    grad_first = jnp.dot(keys_rows.T, grad_gate, preferred_element_type=jnp.float32)
    grad_third = jnp.dot(keys_rows.T, grad_up, preferred_element_type=jnp.float32)
    return (
        renorm(weights[0], grad_first),
        renorm(weights[1], grad_third),
        renorm(weights[2], grad_down),
    )


def inverse_of(permuted):
    count = permuted.shape[0]
    labels = jnp.arange(count, dtype=jnp.int32)
    return jnp.sum(jnp.where(permuted[None, :] == labels[:, None], labels[None, :], 0), axis=1)


def schedule_kernel(levels, lanes, horizon, items_ref, sends_ref, finals_ref):
    problems, _, count = items_ref.shape
    rows = 2 * levels
    shape = (rows, count)
    row = lax.broadcasted_iota(jnp.int32, shape, 0)
    item = lax.broadcasted_iota(jnp.int32, shape, 1)
    right = row < levels
    level = jnp.where(right, row, row - levels)
    heading = jnp.where(right, 1, -1)
    column = lax.broadcasted_iota(jnp.int32, (rows, 128), 1)
    for problem in range(problems):
        source = jnp.broadcast_to(items_ref[problem, 0:1, :], shape)
        target = jnp.broadcast_to(items_ref[problem, 1:2, :], shape)
        lane = jnp.broadcast_to(items_ref[problem, 2:3, :], shape)
        live = jnp.broadcast_to(items_ref[problem, 3:4, :], shape)
        present = jnp.where(level == source, live, 0) * jnp.where((target - source) * heading > 0, 1, 0)
        index = lane
        following = jnp.where(right, level + 1, level - 1)
        urgency = jnp.abs(target - level) * count + item + 1
        final = items_ref[problem, 2:3, :]
        sends = jnp.zeros((rows, 128), jnp.int32)
        for step in range(horizon):
            key = jnp.where(present > 0, urgency, 0)
            best = jnp.max(key, axis=1, keepdims=True)
            chosen = jnp.where((key == best) & (present > 0), 1, 0)
            sent = jnp.sum(chosen * index, axis=1, keepdims=True)
            busy = jnp.sum(chosen, axis=1, keepdims=True)
            sends = jnp.where(column == step, sent, sends)
            sends = jnp.where((column == 127) & (busy > 0), step + 1, sends)
            arrived = jnp.where(target == following, chosen, 0)
            mark = jnp.where(right, lanes + step, lanes + horizon + step)
            landed = jnp.max(arrived * mark, axis=0, keepdims=True)
            final = jnp.where(landed > 0, landed, final)
            moving = chosen - arrived
            moved = pltpu.roll(jnp.where(right, moving, 0), 1, 0)
            moved += pltpu.roll(jnp.where(right, 0, moving), rows - 1, 0)
            present = present - chosen + moved
            index = jnp.where(moved > 0, lanes + step, index)
        left = jnp.max(present, axis=1, keepdims=True)
        sends = jnp.where((column == 127) & (left > 0), horizon + 1, sends)
        sends_ref[problem] = sends
        finals_ref[problem] = final


def plan_routes(levels, lanes, horizon, my_level, sources, targets, live):
    problems, count = targets.shape
    sources = jnp.broadcast_to(sources, targets.shape)
    items = jnp.stack([sources // lanes, targets // lanes, sources % lanes, live], axis=1)
    sends, finals = pl.pallas_call(
        functools.partial(schedule_kernel, levels, lanes, horizon),
        out_shape=(
            jax.ShapeDtypeStruct((problems, 2 * levels, 128), jnp.int32),
            jax.ShapeDtypeStruct((problems, 1, count), jnp.int32),
        ),
        name="plan_routes",
    )(items)
    steps = jnp.max(sends[:, :, 127], axis=1)
    to_right = lax.dynamic_index_in_dim(sends, my_level, 1, keepdims=False)[:, :horizon]
    to_left = lax.dynamic_index_in_dim(sends, levels + my_level, 1, keepdims=False)[:, :horizon]
    kept_by = my_level * lanes + jnp.arange(lanes, dtype=jnp.int32)
    kept = jnp.sum(jnp.where(targets[:, None, :] == kept_by[None, :, None], finals, 0), axis=2)
    return to_right, to_left, kept, steps


def pick_kernel(layout, sizes, *refs):
    index_ref = refs[0]
    ins = refs[1 : 1 + len(sizes)]
    outs = refs[1 + len(sizes) : -1]
    sems = refs[-1]
    candidates = []
    for ref, size in zip(ins, sizes):
        candidates.extend([ref] if size is None else [ref.at[lane] for lane in range(size)])
    slots = []
    for number, (slot_count, allowed) in enumerate(layout):
        for slot in range(max(slot_count, 1)):
            place = outs[number] if slot_count == 0 else outs[number].at[slot]
            slots.append((place, allowed))
    for slot, (place, allowed) in enumerate(slots):
        wanted = index_ref[slot]
        for value, position in allowed:

            @pl.when(wanted == value)
            def _():
                pltpu.make_async_copy(candidates[position], place, sems.at[slot]).start()

    for slot, (place, allowed) in enumerate(slots):
        pltpu.make_async_copy(candidates[allowed[0][1]], place, sems.at[slot]).wait()


def pick(indices, own, arrays, layout):
    item = own.shape[1:]
    sizes = [own.shape[0]] + [None] * len(arrays)
    total = sum(max(slot_count, 1) for slot_count, _ in layout)
    return pl.pallas_call(
        functools.partial(pick_kernel, layout, sizes),
        out_shape=tuple(
            jax.ShapeDtypeStruct(((slot_count,) if slot_count else ()) + item, own.dtype) for slot_count, _ in layout
        ),
        in_specs=[pl.BlockSpec(memory_space=pltpu.SMEM)] + [pl.BlockSpec(memory_space=pl.ANY)] * (1 + len(arrays)),
        out_specs=tuple(pl.BlockSpec(memory_space=pl.ANY) for _ in layout),
        scratch_shapes=[pltpu.SemaphoreType.DMA((total,))],
        name="pick_items",
    )(indices, own, *arrays)


def step_along(own, rights, lefts, step, to_right, to_left, levels):
    lanes = own.shape[0]
    count = len(rights)
    from_own = [(lane, lane) for lane in range(lanes)]
    layout = (
        (0, from_own + [(lanes + t, lanes + t) for t in range(count)]),
        (0, from_own + [(lanes + t, lanes + count + t) for t in range(count)]),
    )
    indices = jnp.stack([to_right[step], to_left[step]])
    out_right, out_left = pick(indices, own, rights + lefts, layout)
    in_right = lax.ppermute(out_right, "z", [(i, i + 1) for i in range(levels - 1)])
    in_left = lax.ppermute(out_left, "z", [(i + 1, i) for i in range(levels - 1)])
    return rights + [in_right], lefts + [in_left]


def settle(own, rights, lefts, kept, horizon):
    lanes = own.shape[0]
    count = len(rights)
    allowed = [(lane, lane) for lane in range(lanes)]
    allowed += [(lanes + t, lanes + t) for t in range(count)]
    allowed += [(lanes + horizon + t, lanes + count + t) for t in range(count)]
    return pick(kept, own, rights + lefts, ((lanes, allowed),))[0]


def route(own, plan, needed, steps, horizon, levels):
    to_right, to_left, kept, origin = plan
    rights, lefts = [], []
    for step in range(steps):
        rights, lefts = step_along(own, rights, lefts, step, to_right, to_left, levels)

    def enough(own, rights, lefts):
        return settle(own, rights, lefts, kept, horizon)

    def more(own, rights, lefts):
        for step in range(steps, horizon):
            rights, lefts = step_along(own, rights, lefts, step, to_right, to_left, levels)
        return settle(own, rights, lefts, kept, horizon)

    def gathered(own, rights, lefts):
        everything = lax.all_gather(own, "z", axis=0, tiled=True)
        return jnp.take(everything, origin, axis=0)

    branch = jnp.where(needed <= steps, 0, jnp.where(needed <= horizon, 1, 2))
    return lax.switch(branch, (enough, more, gathered), own, rights, lefts)


def exchange(pieces, axes):
    return lax.all_to_all(pieces, axes, split_axis=0, concat_axis=0, tiled=True)


def body(state, keys, values, queries, rates, remaining, first_owner, migration):
    levels = lax.axis_size("z")
    lanes = lax.axis_size(LEVEL)
    devices = levels * lanes
    myself = lax.axis_index(GROUP)
    my_level = lax.axis_index("z")
    doc_first = inverse_of(first_owner)
    source_of = inverse_of(migration)
    doc_here = doc_first[myself]
    block_rows, width = keys.shape[2], keys.shape[3]
    part = block_rows // lanes
    weights = (state[0, 0], state[0, 1], state[0, 2])

    steps = (devices // 4 + 1, devices // 8 + 2)
    horizon = steps[0] + EXTRA
    labels = jnp.arange(devices, dtype=jnp.int32)
    targets = jnp.stack([first_owner, first_owner])
    live = jnp.stack([jnp.ones_like(remaining), (remaining >= 2).astype(jnp.int32)])
    to_right, to_left, kept, needed = plan_routes(levels, lanes, horizon, my_level, labels, targets, live)
    origin = lax.dynamic_slice_in_dim(doc_first, my_level * lanes, lanes, 0)

    def deal(blocks):
        split = [block.reshape(lanes, 1, part, width) for block in blocks]
        return exchange(jnp.concatenate(split, axis=1), LEVEL)

    def collect(settled):
        return exchange(settled, LEVEL)

    def bring(section, blocks):
        plan = (to_right[section], to_left[section], kept[section], origin)
        return collect(route(deal(blocks), plan, needed[section], steps[section], horizon, levels))

    def run_round(section, weights_in):
        pair = bring(section, (keys[section, 0], values[section, 0]))
        asked = bring(section, (queries[section, 0],))
        rate_here = lax.dynamic_index_in_dim(rates[section], doc_here, 0, keepdims=False)
        keys_here = pair[:, 0].reshape(block_rows, width)
        values_here = pair[:, 1].reshape(block_rows, width)
        updated = fast_update(weights_in, keys_here, values_here, rate_here)
        return updated, swiglu_apply(updated, asked.reshape(block_rows, width))

    updated, result_one = run_round(0, weights)
    outgoing = result_one.astype(jnp.bfloat16).reshape(devices, block_rows // devices, width)
    dealt_out = exchange(outgoing, GROUP)
    returned = exchange(jnp.take(dealt_out, first_owner, axis=0), GROUP)
    round_one = returned.reshape(1, block_rows, width)

    _, result_two = run_round(1, updated)
    is_live = remaining[doc_here] >= 2
    masked = jnp.where(is_live, result_two, jnp.float32(0.0)).astype(jnp.bfloat16)
    dealt = exchange(masked.reshape(devices, block_rows // devices, width), GROUP)
    regrouped = exchange(jnp.take(dealt, source_of, axis=0), GROUP)
    round_two = regrouped.reshape(1, block_rows, width)
    return (round_one, round_two)


def solution(mesh):
    groups, along, cores = (mesh.shape[name] for name in ("grp", "seq", "doc"))
    wide = max(d for d in range(1, along + 1) if along % d == 0 and d**3 <= along)
    fine = Mesh(mesh.devices.reshape(groups, along // wide, wide, cores), ("grp",) + GROUP)
    everywhere = ("grp",) + GROUP
    return jax.shard_map(
        body,
        mesh=fine,
        in_specs=(
            P(everywhere, None, None, None),
            P(None, everywhere, None, None),
            P(None, everywhere, None, None),
            P(None, everywhere, None, None),
            P(None, "grp", None),
            P("grp"),
            P("grp"),
            P("grp"),
        ),
        out_specs=(P(everywhere, None, None), P(everywhere, None, None)),
        check_vma=False,
    )
```

```python
import functools
import math

import jax
import jax.numpy as jnp
from jax import lax
from jax.experimental import pallas as pl
from jax.experimental.pallas import tpu as pltpu
from jax.sharding import Mesh, PartitionSpec as P

EPSILON = 1e-06
LEVEL = ("x", "core")
GROUP = ("z", "x", "core")
EXTRA = 2
LAG = 2
LONGEST = 16


def dot(left, right, left_dim, right_dim):
    return lax.dot_general(left, right, (((left_dim,), (right_dim,)), ((), ())), preferred_element_type=jnp.float32)


def round_kernel(tiles, live_ref, blocks_ref, rates_ref, first_ref, third_ref, second_ref, *refs):
    result_ref, fresh_ref, stepped_ref, held_ref, turned_ref, values_ref, old_ref, new_ref = refs
    new_first, new_third, new_second = (fresh_ref.at[0, member] for member in range(3))
    lanes, _, part, width = blocks_ref.shape
    rows = lanes * part
    tile = first_ref.shape[-1]
    mean = 1.0 / width
    number = pl.program_id(0)

    def columns_of(index):
        start = index * tile
        return pl.ds(start if isinstance(index, int) else pl.multiple_of(start, tile), tile)

    def block(index):
        return blocks_ref[:, index].reshape(rows, width)

    @pl.when(number == 0)
    def _():
        turned_ref[...] = block(0).T
        values_ref[...] = (rates_ref[...] * block(1).astype(jnp.float32)).astype(jnp.bfloat16)
        old_ref[...] = jnp.zeros_like(old_ref)
        new_ref[...] = jnp.zeros_like(new_ref)

    def renorm(before, gradient):
        before = before.astype(jnp.float32)
        stepped = before - gradient
        old = jnp.sqrt(jnp.sum(before * before, axis=0, keepdims=True) * mean + EPSILON)
        new = jnp.sqrt(jnp.sum(stepped * stepped, axis=0, keepdims=True) * mean + EPSILON)
        return (stepped * (old / new)).astype(jnp.bfloat16)

    columns = columns_of(number)
    first, third, second = first_ref[0, 0], third_ref[0, 0], second_ref[0, 0]
    keys, values = block(0), values_ref[...]
    gate = dot(keys, first, 1, 0)
    upward = dot(keys, third, 1, 0)
    sigmoid = jax.nn.sigmoid(gate)
    active = gate * sigmoid
    hidden = (active * upward).astype(jnp.bfloat16)
    slope = sigmoid * (1.0 + gate * (1.0 - sigmoid))
    grad_hidden = -dot(values, second, 1, 1)
    grad_gate = (grad_hidden * upward * slope).astype(jnp.bfloat16)
    grad_up = (grad_hidden * active).astype(jnp.bfloat16)
    new_first[:, columns] = renorm(first, dot(turned_ref[...], grad_gate, 1, 0))
    new_third[:, columns] = renorm(third, dot(turned_ref[...], grad_up, 1, 0))
    before = second.astype(jnp.float32)
    stepped = before + dot(hidden, values, 0, 0)
    stepped_ref[columns, :] = stepped
    old_ref[...] += jnp.sum(before * before, axis=0, keepdims=True)
    new_ref[...] += jnp.sum(stepped * stepped, axis=0, keepdims=True)

    @pl.when(number == tiles - 1)
    def _():
        factor = jnp.sqrt(old_ref[...] * mean + EPSILON) / jnp.sqrt(new_ref[...] * mean + EPSILON)
        for index in range(tiles):
            columns = columns_of(index)
            new_second[columns, :] = (stepped_ref[columns, :] * factor).astype(jnp.bfloat16)
            gate = dot(block(2), new_first[:, columns], 1, 0)
            upward = dot(block(2), new_third[:, columns], 1, 0)
            held_ref[:, columns] = (gate * jax.nn.sigmoid(gate) * upward).astype(jnp.bfloat16)
        live = live_ref[0] > 0
        for index in range(width // tile):
            columns = columns_of(index)
            out = dot(held_ref[...], new_second[:, columns], 1, 0)
            result_ref[:, columns] = jnp.where(live, out, 0.0).astype(jnp.bfloat16)


def run_document(live, blocks, rates, weights, keep):
    lanes, _, part, width = blocks.shape
    rows = lanes * part
    hidden_width = weights.shape[-1]
    tile = math.gcd(256, hidden_width)
    tiles = hidden_width // tile
    whole = pl.BlockSpec(memory_space=pltpu.VMEM)
    result = jax.ShapeDtypeStruct((rows, width), jnp.bfloat16)
    fresh = (1, 3, hidden_width, width)
    spots = [
        pl.BlockSpec((1, 1, width, tile), lambda i: (0, 0, 0, i)),
        pl.BlockSpec((1, 1, width, tile), lambda i: (0, 1, 0, i)),
        pl.BlockSpec((1, 1, tile, width), lambda i: (0, 2, i, 0)),
    ]
    scratch = [
        pltpu.VMEM((hidden_width, width), jnp.float32),
        pltpu.VMEM((rows, hidden_width), jnp.bfloat16),
        pltpu.VMEM((width, rows), jnp.bfloat16),
        pltpu.VMEM((rows, width), jnp.bfloat16),
        pltpu.VMEM((1, width), jnp.float32),
        pltpu.VMEM((1, width), jnp.float32),
    ]
    if not keep:
        scratch = [pltpu.VMEM(fresh, jnp.bfloat16)] + scratch
    return pl.pallas_call(
        functools.partial(round_kernel, tiles),
        grid=(tiles,),
        in_specs=[pl.BlockSpec(memory_space=pltpu.SMEM), whole, whole] + spots,
        out_specs=(whole,) + ((pl.BlockSpec(fresh, lambda i: (0, 0, 0, 0)),) if keep else ()),
        out_shape=(result,) + ((jax.ShapeDtypeStruct(fresh, jnp.bfloat16),) if keep else ()),
        scratch_shapes=scratch,
        compiler_params=pltpu.CompilerParams(vmem_limit_bytes=36 << 20),
        cost_estimate=pl.CostEstimate(
            flops=18 * rows * width * hidden_width,
            transcendentals=2 * rows * hidden_width,
            bytes_accessed=12 * width * hidden_width + 8 * rows * width,
        ),
        name="run_document",
    )(live.reshape(1), blocks, rates.reshape(rows, 1), weights, weights, weights)


def inverse_of(permuted):
    count = permuted.shape[0]
    labels = jnp.arange(count, dtype=jnp.int32)
    return jnp.sum(jnp.where(permuted[None, :] == labels[:, None], labels[None, :], 0), axis=1)


def schedule_kernel(levels, lanes, horizon, level_ref, items_ref, table_ref):
    problems, _, count = items_ref.shape
    rows = 2 * levels
    shape = (rows, count)
    row = lax.broadcasted_iota(jnp.int32, shape, 0)
    item = lax.broadcasted_iota(jnp.int32, shape, 1)
    right = row < levels
    level = jnp.where(right, row, row - levels)
    heading = jnp.where(right, 1, -1)
    mine = level_ref[0]
    column = lax.broadcasted_iota(jnp.int32, (1, table_ref.shape[2]), 1)
    last = 2 * horizon + lanes
    for problem in range(problems):
        source = jnp.broadcast_to(items_ref[problem, 0:1, :], shape)
        target = jnp.broadcast_to(items_ref[problem, 1:2, :], shape)
        lane = jnp.broadcast_to(items_ref[problem, 2:3, :], shape)
        live = jnp.broadcast_to(items_ref[problem, 4:5, :], shape)
        present = jnp.where(level == source, live, 0) * jnp.where((target - source) * heading > 0, 1, 0)
        index = lane
        following = jnp.where(right, level + 1, level - 1)
        urgency = jnp.abs(target - level) * count + item + 1
        final = items_ref[problem, 2:3, :]
        table = jnp.zeros(column.shape, jnp.int32)
        needed = jnp.zeros((1, 1), jnp.int32)
        for step in range(horizon):
            key = jnp.where(present > 0, urgency, 0)
            best = jnp.max(key, axis=1, keepdims=True)
            chosen = jnp.where((key == best) & (present > 0), 1, 0)
            own_row = jnp.where(row == mine, chosen * index, 0)
            sent_right = jnp.max(jnp.max(own_row, axis=1, keepdims=True), axis=0, keepdims=True)
            own_row = jnp.where(row == levels + mine, chosen * index, 0)
            sent_left = jnp.max(jnp.max(own_row, axis=1, keepdims=True), axis=0, keepdims=True)
            table = jnp.where(column == step, sent_right, table)
            table = jnp.where(column == horizon + step, sent_left, table)
            busy = jnp.max(best, axis=0, keepdims=True)
            needed = jnp.where(busy > 0, step + 1, needed)
            arrived = jnp.where(target == following, chosen, 0)
            mark = jnp.where(right, lanes + step, lanes + horizon + step)
            landed = jnp.max(arrived * mark, axis=0, keepdims=True)
            final = jnp.where(landed > 0, landed, final)
            moving = chosen - arrived
            moved = pltpu.roll(jnp.where(right, moving, 0), 1, 0)
            moved += pltpu.roll(jnp.where(right, 0, moving), rows - 1, 0)
            present = present - chosen + moved
            index = jnp.where(moved > 0, lanes + step, index)
        left = jnp.max(jnp.max(present, axis=1, keepdims=True), axis=0, keepdims=True)
        needed = jnp.where(left > 0, horizon + 1, needed)
        table = jnp.where(column == last, needed, table)
        for lane_here in range(lanes):
            kept = (items_ref[problem, 1:2, :] == mine) & (items_ref[problem, 3:4, :] == lane_here)
            value = jnp.max(jnp.where(kept, final, 0), axis=1, keepdims=True)
            table = jnp.where(column == 2 * horizon + lane_here, value, table)
        table_ref[problem] = table


def plan_routes(levels, lanes, horizon, my_level, targets, live):
    problems, count = targets.shape
    sources = jnp.broadcast_to(jnp.arange(count, dtype=jnp.int32), targets.shape)
    items = jnp.stack([sources // lanes, targets // lanes, sources % lanes, targets % lanes, live], axis=1)
    columns = -(-(2 * horizon + lanes + 1) // 128) * 128
    return pl.pallas_call(
        functools.partial(schedule_kernel, levels, lanes, horizon),
        out_shape=jax.ShapeDtypeStruct((problems, 1, columns), jnp.int32),
        in_specs=[pl.BlockSpec(memory_space=pltpu.SMEM), pl.BlockSpec(memory_space=pltpu.VMEM)],
        name="plan_routes",
    )(my_level.reshape(1), items).reshape(problems, columns)


def pick_kernel(layout, sizes, problem, *refs):
    index_ref = refs[0]
    ins = refs[1 : 1 + len(sizes)]
    outs = refs[1 + len(sizes) : -1]
    sems = refs[-1]
    candidates = []
    for ref, size in zip(ins, sizes):
        candidates.extend([ref] if size is None else [ref.at[lane] for lane in range(size)])
    slots = []
    for number, (slot_count, first, allowed) in enumerate(layout):
        for slot in range(max(slot_count, 1)):
            place = outs[number] if slot_count == 0 else outs[number].at[slot]
            slots.append((place, first + slot, allowed))
    for slot, (place, entry, allowed) in enumerate(slots):
        wanted = index_ref[problem, entry]
        for value, position in allowed:

            @pl.when(wanted == value)
            def _():
                pltpu.make_async_copy(candidates[position], place, sems.at[slot]).start()

    for slot, (place, _, allowed) in enumerate(slots):
        pltpu.make_async_copy(candidates[allowed[0][1]], place, sems.at[slot]).wait()


def pick(table, problem, own, arrays, layout):
    item = own.shape[1:]
    sizes = [own.shape[0]] + [None] * len(arrays)
    total = sum(max(slot_count, 1) for slot_count, _, _ in layout)
    item_bytes = math.prod(item) * own.dtype.itemsize
    return pl.pallas_call(
        functools.partial(pick_kernel, layout, sizes, problem),
        out_shape=tuple(
            jax.ShapeDtypeStruct(((slot_count,) if slot_count else ()) + item, own.dtype) for slot_count, _, _ in layout
        ),
        in_specs=[pl.BlockSpec(memory_space=pltpu.SMEM)] + [pl.BlockSpec(memory_space=pl.ANY)] * (1 + len(arrays)),
        out_specs=tuple(pl.BlockSpec(memory_space=pltpu.VMEM) for _ in layout),
        scratch_shapes=[pltpu.SemaphoreType.DMA((total,))],
        compiler_params=pltpu.CompilerParams(vmem_limit_bytes=16 << 20),
        cost_estimate=pl.CostEstimate(flops=0, transcendentals=0, bytes_accessed=4 * total * item_bytes),
        name="pick_items",
    )(table, own, *arrays)


class Order:
    def __init__(self):
        self.last = ()

    def add(self, *values):
        self.last = values

    def follow(self, value):
        return after(value, *self.last) if self.last else value


def exchange(pieces, axes):
    return lax.all_to_all(pieces, axes, split_axis=0, concat_axis=0, tiled=True)


def spread(own, doc_of, levels):
    lanes, blocks, part, width = own.shape
    pieces = jnp.moveaxis(own.reshape(lanes, blocks, levels, part // levels, width), 2, 0)
    dealt = exchange(pieces, "z").reshape(levels * lanes, blocks, part // levels, width)
    placed = jnp.take(dealt, doc_of, axis=0).reshape(pieces.shape)
    return jnp.moveaxis(exchange(placed, "z"), 0, 2).reshape(own.shape)


class Route:
    def __init__(self, own, table, problem, doc_of, steps, horizon, levels):
        self.own, self.table, self.problem, self.doc_of = own, table, problem, doc_of
        self.steps, self.horizon, self.levels = steps, horizon, levels
        self.rights, self.lefts = [], []

    def step(self, order):
        self.rights, self.lefts = self.stepped(self.rights, self.lefts, self.own, self.table, order)

    def stepped(self, rights, lefts, own, table, order=None):
        ways = (0, [(i, i + 1) for i in range(self.levels - 1)]), (self.horizon, [(i + 1, i) for i in range(self.levels - 1)])
        came = []
        for arrivals, (first, pairs) in zip((rights, lefts), ways):
            lanes, count = own.shape[0], len(arrivals)
            allowed = [(index, index) for index in range(lanes + count)]
            entries = order.follow(table) if order else table
            (outgoing,) = pick(entries, self.problem, own, arrivals, ((0, first + count, allowed),))
            if order:
                order.add(outgoing)
            came.append(arrivals + [lax.ppermute(outgoing, "z", pairs)])
        return came

    def settle(self, rights, lefts, own, table):
        lanes, count = own.shape[0], len(rights)
        allowed = [(lane, lane) for lane in range(lanes)]
        allowed += [(lanes + t, lanes + t) for t in range(count)]
        allowed += [(lanes + self.horizon + t, lanes + count + t) for t in range(count)]
        return pick(table, self.problem, own, rights + lefts, ((lanes, 2 * self.horizon, allowed),))[0]

    def finish(self, rights, lefts, own, table):
        lanes = own.shape[0]

        def more(rights, lefts, own, table):
            if len(rights) == self.horizon:
                return spread(own, self.doc_of, self.levels)
            rights, lefts = self.stepped(rights, lefts, own, table)
            return self.finish(rights, lefts, own, table)

        needed = table[self.problem, 2 * self.horizon + lanes]
        return lax.cond(needed > len(rights), more, self.settle, rights, lefts, own, table)

    def result(self, *earlier):
        table = after(self.table, *earlier) if earlier else self.table
        return self.finish(self.rights, self.lefts, self.own, table)


def pack_kernel(*refs):
    out_ref = refs[-1]
    for number, ref in enumerate(refs[:-1]):
        out_ref[0, number] = ref[0, 0]


def pack(section, lanes, blocks):
    block_rows, width = blocks[0].shape[2:]
    part = block_rows // lanes
    shape = (lanes, len(blocks), part, width)
    return pl.pallas_call(
        pack_kernel,
        grid=(lanes,),
        in_specs=[pl.BlockSpec((1, 1, part, width), lambda lane: (section, 0, lane, 0)) for _ in blocks],
        out_specs=pl.BlockSpec((1,) + shape[1:], lambda lane: (lane, 0, 0, 0)),
        out_shape=jax.ShapeDtypeStruct(shape, blocks[0].dtype),
        cost_estimate=pl.CostEstimate(flops=0, transcendentals=0, bytes_accessed=4 * math.prod(shape)),
        name="pack_blocks",
    )(*blocks)


def after(value, *others):
    return lax.optimization_barrier((value,) + others)[0]


def body(state, keys, values, queries, rates, remaining, first_owner, migration):
    levels = lax.axis_size("z")
    lanes = lax.axis_size(LEVEL)
    devices = levels * lanes
    myself = lax.axis_index(GROUP)
    my_level = lax.axis_index("z")
    block_rows, width = keys.shape[2], keys.shape[3]
    piece_rows = block_rows // devices
    packed_first = pack(0, lanes, (keys, values, queries))
    own_first = exchange(packed_first, LEVEL)

    doc_first = inverse_of(first_owner)
    doc_here = doc_first[myself]
    steps = (devices // 4 + 1, devices // 8 + 1)
    horizon = steps[0] + EXTRA
    has_second = (remaining >= 2).astype(jnp.int32)
    rates_here = lax.dynamic_index_in_dim(rates, doc_here, 1, keepdims=False)
    source_of = inverse_of(migration)
    blocks = (keys, values, queries)

    if horizon > LONGEST:
        own_second = exchange(pack(1, lanes, blocks), LEVEL)
        blocks_first = exchange(spread(own_first, doc_first, levels), LEVEL)
        blocks_second = exchange(spread(own_second, doc_first, levels), LEVEL)
    else:
        targets = jnp.stack([first_owner, first_owner])
        live = jnp.stack([jnp.ones_like(has_second), has_second])
        table = plan_routes(levels, lanes, horizon, my_level, targets, live)
        first = Route(own_first, table, 0, doc_first, steps[0], horizon, levels)
        order = Order()
        first.step(order)
        own_second = exchange(order.follow(after(pack(1, lanes, blocks), table)), LEVEL)
        second = Route(own_second, table, 1, doc_first, steps[1], horizon, levels)
        for step in range(1, max(steps[0], steps[1] + LAG)):
            if step >= LAG and step - LAG < steps[1]:
                second.step(order)
            if step < steps[0]:
                first.step(order)
        blocks_first = exchange(first.result(second.rights[-1], second.lefts[-1]), LEVEL)
        blocks_second = exchange(second.result(), LEVEL)

    always = jnp.ones((), jnp.int32)
    result_one, updated = run_document(always, blocks_first, rates_here[0], state, True)
    dealt_one = exchange(result_one.reshape(devices, piece_rows, width), GROUP)
    (result_two,) = run_document(has_second[doc_here], blocks_second, rates_here[1], updated, False)
    both = jnp.stack([jnp.take(dealt_one, first_owner, axis=0), result_two.reshape(devices, piece_rows, width)], axis=1)
    both = exchange(both, GROUP)
    round_one, dealt_two = both[:, 0], both[:, 1]
    round_two = exchange(jnp.take(dealt_two, source_of, axis=0), GROUP)
    return round_one.reshape(1, block_rows, width), round_two.reshape(1, block_rows, width)


def solution(mesh):
    groups, along, cores = (mesh.shape[name] for name in ("grp", "seq", "doc"))
    wide = max(d for d in range(1, along + 1) if along % d == 0 and d**3 <= along)
    fine = Mesh(mesh.devices.reshape(groups, along // wide, wide, cores), ("grp",) + GROUP)
    everywhere = ("grp",) + GROUP
    return jax.shard_map(
        body,
        mesh=fine,
        in_specs=(
            P(everywhere, None, None, None),
            P(None, everywhere, None, None),
            P(None, everywhere, None, None),
            P(None, everywhere, None, None),
            P(None, "grp", None),
            P("grp"),
            P("grp"),
            P("grp"),
        ),
        out_specs=(P(everywhere, None, None), P(everywhere, None, None)),
        check_vma=False,
    )
```

```python
import functools
import math

import jax
import jax.numpy as jnp
from jax import lax
from jax.experimental import pallas as pl
from jax.experimental.pallas import tpu as pltpu
from jax.sharding import Mesh, PartitionSpec as P

EPSILON = 1e-06
LEVEL = ("x", "core")
GROUP = ("z", "x", "core")
EXTRA = 2
LAG = 2
LONGEST = 16


def dot(left, right, left_dim, right_dim):
    return lax.dot_general(left, right, (((left_dim,), (right_dim,)), ((), ())), preferred_element_type=jnp.float32)


def round_kernel(tiles, live_ref, blocks_ref, rates_ref, first_ref, third_ref, second_ref, *refs):
    result_ref, fresh_ref, stepped_ref, held_ref, turned_ref, values_ref, old_ref, new_ref = refs
    new_first, new_third, new_second = (fresh_ref.at[0, member] for member in range(3))
    lanes, _, part, width = blocks_ref.shape
    rows = lanes * part
    tile = first_ref.shape[-1]
    mean = 1.0 / width
    number = pl.program_id(0)

    def columns_of(index):
        start = index * tile
        return pl.ds(start if isinstance(index, int) else pl.multiple_of(start, tile), tile)

    def block(index):
        return blocks_ref[:, index].reshape(rows, width)

    @pl.when(number == 0)
    def _():
        turned_ref[...] = block(0).T
        values_ref[...] = (rates_ref[...] * block(1).astype(jnp.float32)).astype(jnp.bfloat16)
        old_ref[...] = jnp.zeros_like(old_ref)
        new_ref[...] = jnp.zeros_like(new_ref)

    def renorm(before, gradient):
        before = before.astype(jnp.float32)
        stepped = before - gradient
        old = jnp.sqrt(jnp.sum(before * before, axis=0, keepdims=True) * mean + EPSILON)
        new = jnp.sqrt(jnp.sum(stepped * stepped, axis=0, keepdims=True) * mean + EPSILON)
        return (stepped * (old / new)).astype(jnp.bfloat16)

    columns = columns_of(number)
    first, third, second = first_ref[0, 0], third_ref[0, 0], second_ref[0, 0]
    keys, values = block(0), values_ref[...]
    gate = dot(keys, first, 1, 0)
    upward = dot(keys, third, 1, 0)
    sigmoid = jax.nn.sigmoid(gate)
    active = gate * sigmoid
    hidden = (active * upward).astype(jnp.bfloat16)
    slope = sigmoid * (1.0 + gate * (1.0 - sigmoid))
    grad_hidden = -dot(values, second, 1, 1)
    grad_gate = (grad_hidden * upward * slope).astype(jnp.bfloat16)
    grad_up = (grad_hidden * active).astype(jnp.bfloat16)
    new_first[:, columns] = renorm(first, dot(turned_ref[...], grad_gate, 1, 0))
    new_third[:, columns] = renorm(third, dot(turned_ref[...], grad_up, 1, 0))
    before = second.astype(jnp.float32)
    stepped = before + dot(hidden, values, 0, 0)
    stepped_ref[columns, :] = stepped
    old_ref[...] += jnp.sum(before * before, axis=0, keepdims=True)
    new_ref[...] += jnp.sum(stepped * stepped, axis=0, keepdims=True)

    @pl.when(number == tiles - 1)
    def _():
        factor = jnp.sqrt(old_ref[...] * mean + EPSILON) / jnp.sqrt(new_ref[...] * mean + EPSILON)
        for index in range(tiles):
            columns = columns_of(index)
            new_second[columns, :] = (stepped_ref[columns, :] * factor).astype(jnp.bfloat16)
            gate = dot(block(2), new_first[:, columns], 1, 0)
            upward = dot(block(2), new_third[:, columns], 1, 0)
            held_ref[:, columns] = (gate * jax.nn.sigmoid(gate) * upward).astype(jnp.bfloat16)
        live = live_ref[0] > 0
        for index in range(width // tile):
            columns = columns_of(index)
            out = dot(held_ref[...], new_second[:, columns], 1, 0)
            result_ref[:, columns] = jnp.where(live, out, 0.0).astype(jnp.bfloat16)


def run_document(live, blocks, rates, weights, keep):
    lanes, _, part, width = blocks.shape
    rows = lanes * part
    hidden_width = weights.shape[-1]
    tile = math.gcd(256, hidden_width)
    tiles = hidden_width // tile
    whole = pl.BlockSpec(memory_space=pltpu.VMEM)
    result = jax.ShapeDtypeStruct((rows, width), jnp.bfloat16)
    fresh = (1, 3, hidden_width, width)
    spots = [
        pl.BlockSpec((1, 1, width, tile), lambda i: (0, 0, 0, i)),
        pl.BlockSpec((1, 1, width, tile), lambda i: (0, 1, 0, i)),
        pl.BlockSpec((1, 1, tile, width), lambda i: (0, 2, i, 0)),
    ]
    scratch = [
        pltpu.VMEM((hidden_width, width), jnp.float32),
        pltpu.VMEM((rows, hidden_width), jnp.bfloat16),
        pltpu.VMEM((width, rows), jnp.bfloat16),
        pltpu.VMEM((rows, width), jnp.bfloat16),
        pltpu.VMEM((1, width), jnp.float32),
        pltpu.VMEM((1, width), jnp.float32),
    ]
    if not keep:
        scratch = [pltpu.VMEM(fresh, jnp.bfloat16)] + scratch
    return pl.pallas_call(
        functools.partial(round_kernel, tiles),
        grid=(tiles,),
        in_specs=[pl.BlockSpec(memory_space=pltpu.SMEM), whole, whole] + spots,
        out_specs=(whole,) + ((pl.BlockSpec(fresh, lambda i: (0, 0, 0, 0)),) if keep else ()),
        out_shape=(result,) + ((jax.ShapeDtypeStruct(fresh, jnp.bfloat16),) if keep else ()),
        scratch_shapes=scratch,
        compiler_params=pltpu.CompilerParams(vmem_limit_bytes=36 << 20),
        cost_estimate=pl.CostEstimate(
            flops=18 * rows * width * hidden_width,
            transcendentals=2 * rows * hidden_width,
            bytes_accessed=12 * width * hidden_width + 8 * rows * width,
        ),
        name="run_document",
    )(live.reshape(1), blocks, rates.reshape(rows, 1), weights, weights, weights)


def inverse_of(permuted):
    count = permuted.shape[0]
    labels = jnp.arange(count, dtype=jnp.int32)
    return jnp.sum(jnp.where(permuted[None, :] == labels[:, None], labels[None, :], 0), axis=1)


def schedule_kernel(levels, lanes, horizon, level_ref, items_ref, table_ref):
    problems, _, count = items_ref.shape
    rows = 2 * levels
    shape = (rows, count)
    row = lax.broadcasted_iota(jnp.int32, shape, 0)
    item = lax.broadcasted_iota(jnp.int32, shape, 1)
    right = row < levels
    level = jnp.where(right, row, row - levels)
    heading = jnp.where(right, 1, -1)
    mine = level_ref[0]
    column = lax.broadcasted_iota(jnp.int32, (1, table_ref.shape[2]), 1)
    last = 2 * horizon + lanes
    for problem in range(problems):
        source = jnp.broadcast_to(items_ref[problem, 0:1, :], shape)
        target = jnp.broadcast_to(items_ref[problem, 1:2, :], shape)
        lane = jnp.broadcast_to(items_ref[problem, 2:3, :], shape)
        live = jnp.broadcast_to(items_ref[problem, 4:5, :], shape)
        present = jnp.where(level == source, live, 0) * jnp.where((target - source) * heading > 0, 1, 0)
        index = lane
        following = jnp.where(right, level + 1, level - 1)
        urgency = jnp.abs(target - level) * count + item + 1
        final = items_ref[problem, 2:3, :]
        table = jnp.zeros(column.shape, jnp.int32)
        needed = jnp.zeros((1, 1), jnp.int32)
        for step in range(horizon):
            key = jnp.where(present > 0, urgency, 0)
            best = jnp.max(key, axis=1, keepdims=True)
            chosen = jnp.where((key == best) & (present > 0), 1, 0)
            own_row = jnp.where(row == mine, chosen * index, 0)
            sent_right = jnp.max(jnp.max(own_row, axis=1, keepdims=True), axis=0, keepdims=True)
            own_row = jnp.where(row == levels + mine, chosen * index, 0)
            sent_left = jnp.max(jnp.max(own_row, axis=1, keepdims=True), axis=0, keepdims=True)
            table = jnp.where(column == step, sent_right, table)
            table = jnp.where(column == horizon + step, sent_left, table)
            busy = jnp.max(best, axis=0, keepdims=True)
            needed = jnp.where(busy > 0, step + 1, needed)
            arrived = jnp.where(target == following, chosen, 0)
            mark = jnp.where(right, lanes + step, lanes + horizon + step)
            landed = jnp.max(arrived * mark, axis=0, keepdims=True)
            final = jnp.where(landed > 0, landed, final)
            moving = chosen - arrived
            moved = pltpu.roll(jnp.where(right, moving, 0), 1, 0)
            moved += pltpu.roll(jnp.where(right, 0, moving), rows - 1, 0)
            present = present - chosen + moved
            index = jnp.where(moved > 0, lanes + step, index)
        left = jnp.max(jnp.max(present, axis=1, keepdims=True), axis=0, keepdims=True)
        needed = jnp.where(left > 0, horizon + 1, needed)
        table = jnp.where(column == last, needed, table)
        for lane_here in range(lanes):
            kept = (items_ref[problem, 1:2, :] == mine) & (items_ref[problem, 3:4, :] == lane_here)
            value = jnp.max(jnp.where(kept, final, 0), axis=1, keepdims=True)
            table = jnp.where(column == 2 * horizon + lane_here, value, table)
        table_ref[problem] = table


def plan_routes(levels, lanes, horizon, my_level, targets, live):
    problems, count = targets.shape
    sources = jnp.broadcast_to(jnp.arange(count, dtype=jnp.int32), targets.shape)
    items = jnp.stack([sources // lanes, targets // lanes, sources % lanes, targets % lanes, live], axis=1)
    columns = -(-(2 * horizon + lanes + 1) // 128) * 128
    return pl.pallas_call(
        functools.partial(schedule_kernel, levels, lanes, horizon),
        out_shape=jax.ShapeDtypeStruct((problems, 1, columns), jnp.int32),
        in_specs=[pl.BlockSpec(memory_space=pltpu.SMEM), pl.BlockSpec(memory_space=pltpu.VMEM)],
        name="plan_routes",
    )(my_level.reshape(1), items).reshape(problems, columns)


def pick_kernel(layout, sizes, problem, *refs):
    index_ref = refs[0]
    ins = refs[1 : 1 + len(sizes)]
    outs = refs[1 + len(sizes) : -1]
    sems = refs[-1]
    candidates = []
    for ref, size in zip(ins, sizes):
        candidates.extend([ref] if size is None else [ref.at[lane] for lane in range(size)])
    slots = []
    for number, (slot_count, first, allowed) in enumerate(layout):
        for slot in range(max(slot_count, 1)):
            place = outs[number] if slot_count == 0 else outs[number].at[slot]
            slots.append((place, first + slot, allowed))
    for slot, (place, entry, allowed) in enumerate(slots):
        wanted = index_ref[problem, entry]
        for value, position in allowed:

            @pl.when(wanted == value)
            def _():
                pltpu.make_async_copy(candidates[position], place, sems.at[slot]).start()

    for slot, (place, _, allowed) in enumerate(slots):
        pltpu.make_async_copy(candidates[allowed[0][1]], place, sems.at[slot]).wait()


def pick(table, problem, own, arrays, layout):
    item = own.shape[1:]
    sizes = [own.shape[0]] + [None] * len(arrays)
    total = sum(max(slot_count, 1) for slot_count, _, _ in layout)
    item_bytes = math.prod(item) * own.dtype.itemsize
    return pl.pallas_call(
        functools.partial(pick_kernel, layout, sizes, problem),
        out_shape=tuple(
            jax.ShapeDtypeStruct(((slot_count,) if slot_count else ()) + item, own.dtype) for slot_count, _, _ in layout
        ),
        in_specs=[pl.BlockSpec(memory_space=pltpu.SMEM)] + [pl.BlockSpec(memory_space=pl.ANY)] * (1 + len(arrays)),
        out_specs=tuple(pl.BlockSpec(memory_space=pltpu.VMEM) for _ in layout),
        scratch_shapes=[pltpu.SemaphoreType.DMA((total,))],
        compiler_params=pltpu.CompilerParams(vmem_limit_bytes=16 << 20),
        cost_estimate=pl.CostEstimate(flops=0, transcendentals=0, bytes_accessed=4 * total * item_bytes),
        name="pick_items",
    )(table, own, *arrays)


class Order:
    def __init__(self):
        self.last = ()

    def add(self, *values):
        self.last = values

    def follow(self, value):
        return after(value, *self.last) if self.last else value


def exchange(pieces, axes):
    return lax.all_to_all(pieces, axes, split_axis=0, concat_axis=0, tiled=True)


def spread(own, doc_of, levels):
    lanes, blocks, part, width = own.shape
    pieces = jnp.moveaxis(own.reshape(lanes, blocks, levels, part // levels, width), 2, 0)
    dealt = exchange(pieces, "z").reshape(levels * lanes, blocks, part // levels, width)
    placed = jnp.take(dealt, doc_of, axis=0).reshape(pieces.shape)
    return jnp.moveaxis(exchange(placed, "z"), 0, 2).reshape(own.shape)


class Route:
    def __init__(self, own, table, problem, origin, steps, horizon, levels):
        self.own, self.table, self.problem, self.origin = own, table, problem, origin
        self.steps, self.horizon, self.levels = steps, horizon, levels
        self.rights, self.lefts = [], []

    def step(self, order):
        self.rights, self.lefts = self.stepped(self.rights, self.lefts, self.own, self.table, order)

    def stepped(self, rights, lefts, own, table, order=None):
        ways = (0, [(i, i + 1) for i in range(self.levels - 1)]), (self.horizon, [(i + 1, i) for i in range(self.levels - 1)])
        came = []
        for arrivals, (first, pairs) in zip((rights, lefts), ways):
            lanes, count = own.shape[0], len(arrivals)
            allowed = [(index, index) for index in range(lanes + count)]
            entries = order.follow(table) if order else table
            (outgoing,) = pick(entries, self.problem, own, arrivals, ((0, first + count, allowed),))
            if order:
                order.add(outgoing)
            came.append(arrivals + [lax.ppermute(outgoing, "z", pairs)])
        return came

    def settle(self, rights, lefts, own, table):
        lanes, count = own.shape[0], len(rights)
        allowed = [(lane, lane) for lane in range(lanes)]
        allowed += [(lanes + t, lanes + t) for t in range(count)]
        allowed += [(lanes + self.horizon + t, lanes + count + t) for t in range(count)]
        return pick(table, self.problem, own, rights + lefts, ((lanes, 2 * self.horizon, allowed),))[0]

    def finish(self, rights, lefts, own, table):
        lanes = own.shape[0]

        def more(rights, lefts, own, table):
            if len(rights) == self.horizon:
                everything = lax.all_gather(own, "z", axis=0, tiled=True)
                return jnp.take(everything, self.origin, axis=0)
            rights, lefts = self.stepped(rights, lefts, own, table)
            return self.finish(rights, lefts, own, table)

        needed = table[self.problem, 2 * self.horizon + lanes]
        return lax.cond(needed > len(rights), more, self.settle, rights, lefts, own, table)

    def result(self, *earlier):
        table = after(self.table, *earlier) if earlier else self.table
        return self.finish(self.rights, self.lefts, self.own, table)


def pack_kernel(*refs):
    out_ref = refs[-1]
    for number, ref in enumerate(refs[:-1]):
        out_ref[0, number] = ref[0, 0]


def pack(section, lanes, blocks):
    block_rows, width = blocks[0].shape[2:]
    part = block_rows // lanes
    shape = (lanes, len(blocks), part, width)
    return pl.pallas_call(
        pack_kernel,
        grid=(lanes,),
        in_specs=[pl.BlockSpec((1, 1, part, width), lambda lane: (section, 0, lane, 0)) for _ in blocks],
        out_specs=pl.BlockSpec((1,) + shape[1:], lambda lane: (lane, 0, 0, 0)),
        out_shape=jax.ShapeDtypeStruct(shape, blocks[0].dtype),
        cost_estimate=pl.CostEstimate(flops=0, transcendentals=0, bytes_accessed=4 * math.prod(shape)),
        name="pack_blocks",
    )(*blocks)


def after(value, *others):
    return lax.optimization_barrier((value,) + others)[0]


def body(state, keys, values, queries, rates, remaining, first_owner, migration):
    levels = lax.axis_size("z")
    lanes = lax.axis_size(LEVEL)
    devices = levels * lanes
    myself = lax.axis_index(GROUP)
    my_level = lax.axis_index("z")
    block_rows, width = keys.shape[2], keys.shape[3]
    piece_rows = block_rows // devices
    packed_first = pack(0, lanes, (keys, values, queries))
    own_first = exchange(packed_first, LEVEL)

    doc_first = inverse_of(first_owner)
    doc_here = doc_first[myself]
    steps = (devices // 4 + 1, devices // 8 + 1)
    horizon = steps[0] + EXTRA
    has_second = (remaining >= 2).astype(jnp.int32)
    rates_here = lax.dynamic_index_in_dim(rates, doc_here, 1, keepdims=False)
    source_of = inverse_of(migration)
    blocks = (keys, values, queries)

    if horizon > LONGEST:
        own_second = exchange(pack(1, lanes, blocks), LEVEL)
        blocks_first = exchange(spread(own_first, doc_first, levels), LEVEL)
        blocks_second = exchange(spread(own_second, doc_first, levels), LEVEL)
    else:
        origin = lax.dynamic_slice_in_dim(doc_first, my_level * lanes, lanes, 0)
        targets = jnp.stack([first_owner, first_owner])
        live = jnp.stack([jnp.ones_like(has_second), has_second])
        table = plan_routes(levels, lanes, horizon, my_level, targets, live)
        first = Route(own_first, table, 0, origin, steps[0], horizon, levels)
        order = Order()
        first.step(order)
        own_second = exchange(order.follow(after(pack(1, lanes, blocks), table)), LEVEL)
        second = Route(own_second, table, 1, origin, steps[1], horizon, levels)
        for step in range(1, max(steps[0], steps[1] + LAG)):
            if step >= LAG and step - LAG < steps[1]:
                second.step(order)
            if step < steps[0]:
                first.step(order)
        blocks_first = exchange(first.result(second.rights[-1], second.lefts[-1]), LEVEL)
        blocks_second = exchange(second.result(), LEVEL)

    always = jnp.ones((), jnp.int32)
    result_one, updated = run_document(always, blocks_first, rates_here[0], state, True)
    dealt_one = exchange(result_one.reshape(devices, piece_rows, width), GROUP)
    (result_two,) = run_document(has_second[doc_here], blocks_second, rates_here[1], updated, False)
    both = jnp.stack([jnp.take(dealt_one, first_owner, axis=0), result_two.reshape(devices, piece_rows, width)], axis=1)
    both = exchange(both, GROUP)
    round_one, dealt_two = both[:, 0], both[:, 1]
    round_two = exchange(jnp.take(dealt_two, source_of, axis=0), GROUP)
    return round_one.reshape(1, block_rows, width), round_two.reshape(1, block_rows, width)


def solution(mesh):
    groups, along, cores = (mesh.shape[name] for name in ("grp", "seq", "doc"))
    wide = max(d for d in range(1, along + 1) if along % d == 0 and d**3 <= along)
    fine = Mesh(mesh.devices.reshape(groups, along // wide, wide, cores), ("grp",) + GROUP)
    everywhere = ("grp",) + GROUP
    return jax.shard_map(
        body,
        mesh=fine,
        in_specs=(
            P(everywhere, None, None, None),
            P(None, everywhere, None, None),
            P(None, everywhere, None, None),
            P(None, everywhere, None, None),
            P(None, "grp", None),
            P("grp"),
            P("grp"),
            P("grp"),
        ),
        out_specs=(P(everywhere, None, None), P(everywhere, None, None)),
        check_vma=False,
    )
```

```python
import functools
import math

import jax
import jax.numpy as jnp
from jax import lax
from jax.experimental import pallas as pl
from jax.experimental.pallas import tpu as pltpu
from jax.sharding import Mesh, PartitionSpec as P

EPSILON = 1e-06
LEVEL = ("x", "core")
GROUP = ("z", "x", "core")
EXTRA = 2
LAG = 2
LONGEST = 16


def dot(left, right, left_dim, right_dim):
    return lax.dot_general(left, right, (((left_dim,), (right_dim,)), ((), ())), preferred_element_type=jnp.float32)


def round_kernel(tiles, live_ref, blocks_ref, rates_ref, first_ref, third_ref, second_ref, *refs):
    result_ref, fresh_ref, stepped_ref, held_ref, turned_ref, values_ref, old_ref, new_ref = refs
    new_first, new_third, new_second = (fresh_ref.at[0, member] for member in range(3))
    lanes, _, part, width = blocks_ref.shape
    rows = lanes * part
    tile = first_ref.shape[-1]
    mean = 1.0 / width
    number = pl.program_id(0)

    def columns_of(index):
        start = index * tile
        return pl.ds(start if isinstance(index, int) else pl.multiple_of(start, tile), tile)

    def block(index):
        return blocks_ref[:, index].reshape(rows, width)

    @pl.when(number == 0)
    def _():
        turned_ref[...] = block(0).T
        values_ref[...] = (rates_ref[...] * block(1).astype(jnp.float32)).astype(jnp.bfloat16)
        old_ref[...] = jnp.zeros_like(old_ref)
        new_ref[...] = jnp.zeros_like(new_ref)

    def renorm(before, gradient):
        before = before.astype(jnp.float32)
        stepped = before - gradient
        old = jnp.sqrt(jnp.sum(before * before, axis=0, keepdims=True) * mean + EPSILON)
        new = jnp.sqrt(jnp.sum(stepped * stepped, axis=0, keepdims=True) * mean + EPSILON)
        return (stepped * (old / new)).astype(jnp.bfloat16)

    columns = columns_of(number)
    first, third, second = first_ref[0, 0], third_ref[0, 0], second_ref[0, 0]
    keys, values = block(0), values_ref[...]
    gate = dot(keys, first, 1, 0)
    upward = dot(keys, third, 1, 0)
    sigmoid = jax.nn.sigmoid(gate)
    active = gate * sigmoid
    hidden = (active * upward).astype(jnp.bfloat16)
    slope = sigmoid * (1.0 + gate * (1.0 - sigmoid))
    grad_hidden = -dot(values, second, 1, 1)
    grad_gate = (grad_hidden * upward * slope).astype(jnp.bfloat16)
    grad_up = (grad_hidden * active).astype(jnp.bfloat16)
    new_first[:, columns] = renorm(first, dot(turned_ref[...], grad_gate, 1, 0))
    new_third[:, columns] = renorm(third, dot(turned_ref[...], grad_up, 1, 0))
    before = second.astype(jnp.float32)
    stepped = before + dot(hidden, values, 0, 0)
    stepped_ref[columns, :] = stepped
    old_ref[...] += jnp.sum(before * before, axis=0, keepdims=True)
    new_ref[...] += jnp.sum(stepped * stepped, axis=0, keepdims=True)

    @pl.when(number == tiles - 1)
    def _():
        factor = jnp.sqrt(old_ref[...] * mean + EPSILON) / jnp.sqrt(new_ref[...] * mean + EPSILON)
        for index in range(tiles):
            columns = columns_of(index)
            new_second[columns, :] = (stepped_ref[columns, :] * factor).astype(jnp.bfloat16)
            gate = dot(block(2), new_first[:, columns], 1, 0)
            upward = dot(block(2), new_third[:, columns], 1, 0)
            held_ref[:, columns] = (gate * jax.nn.sigmoid(gate) * upward).astype(jnp.bfloat16)
        live = live_ref[0] > 0
        for index in range(width // tile):
            columns = columns_of(index)
            out = dot(held_ref[...], new_second[:, columns], 1, 0)
            result_ref[:, columns] = jnp.where(live, out, 0.0).astype(jnp.bfloat16)


def run_document(live, blocks, rates, weights, keep):
    lanes, _, part, width = blocks.shape
    rows = lanes * part
    hidden_width = weights.shape[-1]
    tile = math.gcd(256, hidden_width)
    tiles = hidden_width // tile
    whole = pl.BlockSpec(memory_space=pltpu.VMEM)
    result = jax.ShapeDtypeStruct((rows, width), jnp.bfloat16)
    fresh = (1, 3, hidden_width, width)
    spots = [
        pl.BlockSpec((1, 1, width, tile), lambda i: (0, 0, 0, i)),
        pl.BlockSpec((1, 1, width, tile), lambda i: (0, 1, 0, i)),
        pl.BlockSpec((1, 1, tile, width), lambda i: (0, 2, i, 0)),
    ]
    scratch = [
        pltpu.VMEM((hidden_width, width), jnp.float32),
        pltpu.VMEM((rows, hidden_width), jnp.bfloat16),
        pltpu.VMEM((width, rows), jnp.bfloat16),
        pltpu.VMEM((rows, width), jnp.bfloat16),
        pltpu.VMEM((1, width), jnp.float32),
        pltpu.VMEM((1, width), jnp.float32),
    ]
    if not keep:
        scratch = [pltpu.VMEM(fresh, jnp.bfloat16)] + scratch
    return pl.pallas_call(
        functools.partial(round_kernel, tiles),
        grid=(tiles,),
        in_specs=[pl.BlockSpec(memory_space=pltpu.SMEM), whole, whole] + spots,
        out_specs=(whole,) + ((pl.BlockSpec(fresh, lambda i: (0, 0, 0, 0)),) if keep else ()),
        out_shape=(result,) + ((jax.ShapeDtypeStruct(fresh, jnp.bfloat16),) if keep else ()),
        scratch_shapes=scratch,
        compiler_params=pltpu.CompilerParams(vmem_limit_bytes=36 << 20),
        cost_estimate=pl.CostEstimate(
            flops=18 * rows * width * hidden_width,
            transcendentals=2 * rows * hidden_width,
            bytes_accessed=12 * width * hidden_width + 8 * rows * width,
        ),
        name="run_document",
    )(live.reshape(1), blocks, rates.reshape(rows, 1), weights, weights, weights)


def inverse_of(permuted):
    count = permuted.shape[0]
    labels = jnp.arange(count, dtype=jnp.int32)
    return jnp.sum(jnp.where(permuted[None, :] == labels[:, None], labels[None, :], 0), axis=1)


def schedule_kernel(levels, lanes, horizon, level_ref, items_ref, table_ref):
    problems, _, count = items_ref.shape
    rows = 2 * levels
    shape = (rows, count)
    row = lax.broadcasted_iota(jnp.int32, shape, 0)
    item = lax.broadcasted_iota(jnp.int32, shape, 1)
    right = row < levels
    level = jnp.where(right, row, row - levels)
    heading = jnp.where(right, 1, -1)
    mine = level_ref[0]
    column = lax.broadcasted_iota(jnp.int32, (1, table_ref.shape[2]), 1)
    last = 2 * horizon + lanes
    for problem in range(problems):
        source = jnp.broadcast_to(items_ref[problem, 0:1, :], shape)
        target = jnp.broadcast_to(items_ref[problem, 1:2, :], shape)
        lane = jnp.broadcast_to(items_ref[problem, 2:3, :], shape)
        live = jnp.broadcast_to(items_ref[problem, 4:5, :], shape)
        present = jnp.where(level == source, live, 0) * jnp.where((target - source) * heading > 0, 1, 0)
        index = lane
        following = jnp.where(right, level + 1, level - 1)
        urgency = jnp.abs(target - level) * count + item + 1
        final = items_ref[problem, 2:3, :]
        table = jnp.zeros(column.shape, jnp.int32)
        needed = jnp.zeros((1, 1), jnp.int32)
        for step in range(horizon):
            key = jnp.where(present > 0, urgency, 0)
            best = jnp.max(key, axis=1, keepdims=True)
            chosen = jnp.where((key == best) & (present > 0), 1, 0)
            own_row = jnp.where(row == mine, chosen * index, 0)
            sent_right = jnp.max(jnp.max(own_row, axis=1, keepdims=True), axis=0, keepdims=True)
            own_row = jnp.where(row == levels + mine, chosen * index, 0)
            sent_left = jnp.max(jnp.max(own_row, axis=1, keepdims=True), axis=0, keepdims=True)
            table = jnp.where(column == step, sent_right, table)
            table = jnp.where(column == horizon + step, sent_left, table)
            busy = jnp.max(best, axis=0, keepdims=True)
            needed = jnp.where(busy > 0, step + 1, needed)
            arrived = jnp.where(target == following, chosen, 0)
            mark = jnp.where(right, lanes + step, lanes + horizon + step)
            landed = jnp.max(arrived * mark, axis=0, keepdims=True)
            final = jnp.where(landed > 0, landed, final)
            moving = chosen - arrived
            moved = pltpu.roll(jnp.where(right, moving, 0), 1, 0)
            moved += pltpu.roll(jnp.where(right, 0, moving), rows - 1, 0)
            present = present - chosen + moved
            index = jnp.where(moved > 0, lanes + step, index)
        left = jnp.max(jnp.max(present, axis=1, keepdims=True), axis=0, keepdims=True)
        needed = jnp.where(left > 0, horizon + 1, needed)
        table = jnp.where(column == last, needed, table)
        for lane_here in range(lanes):
            kept = (items_ref[problem, 1:2, :] == mine) & (items_ref[problem, 3:4, :] == lane_here)
            value = jnp.max(jnp.where(kept, final, 0), axis=1, keepdims=True)
            table = jnp.where(column == 2 * horizon + lane_here, value, table)
        table_ref[problem] = table


def plan_routes(levels, lanes, horizon, my_level, targets, live):
    problems, count = targets.shape
    sources = jnp.broadcast_to(jnp.arange(count, dtype=jnp.int32), targets.shape)
    items = jnp.stack([sources // lanes, targets // lanes, sources % lanes, targets % lanes, live], axis=1)
    columns = -(-(2 * horizon + lanes + 1) // 128) * 128
    return pl.pallas_call(
        functools.partial(schedule_kernel, levels, lanes, horizon),
        out_shape=jax.ShapeDtypeStruct((problems, 1, columns), jnp.int32),
        in_specs=[pl.BlockSpec(memory_space=pltpu.SMEM), pl.BlockSpec(memory_space=pltpu.VMEM)],
        name="plan_routes",
    )(my_level.reshape(1), items).reshape(problems, columns)


def pick_kernel(layout, sizes, problem, *refs):
    index_ref = refs[0]
    ins = refs[1 : 1 + len(sizes)]
    outs = refs[1 + len(sizes) : -1]
    sems = refs[-1]
    candidates = []
    for ref, size in zip(ins, sizes):
        candidates.extend([ref] if size is None else [ref.at[lane] for lane in range(size)])
    slots = []
    for number, (slot_count, first, allowed) in enumerate(layout):
        for slot in range(max(slot_count, 1)):
            place = outs[number] if slot_count == 0 else outs[number].at[slot]
            slots.append((place, first + slot, allowed))
    for slot, (place, entry, allowed) in enumerate(slots):
        wanted = index_ref[problem, entry]
        for value, position in allowed:

            @pl.when(wanted == value)
            def _():
                pltpu.make_async_copy(candidates[position], place, sems.at[slot]).start()

    for slot, (place, _, allowed) in enumerate(slots):
        pltpu.make_async_copy(candidates[allowed[0][1]], place, sems.at[slot]).wait()


def pick(table, problem, own, arrays, layout):
    item = own.shape[1:]
    sizes = [own.shape[0]] + [None] * len(arrays)
    total = sum(max(slot_count, 1) for slot_count, _, _ in layout)
    item_bytes = math.prod(item) * own.dtype.itemsize
    return pl.pallas_call(
        functools.partial(pick_kernel, layout, sizes, problem),
        out_shape=tuple(
            jax.ShapeDtypeStruct(((slot_count,) if slot_count else ()) + item, own.dtype) for slot_count, _, _ in layout
        ),
        in_specs=[pl.BlockSpec(memory_space=pltpu.SMEM)] + [pl.BlockSpec(memory_space=pl.ANY)] * (1 + len(arrays)),
        out_specs=tuple(pl.BlockSpec(memory_space=pltpu.VMEM) for _ in layout),
        scratch_shapes=[pltpu.SemaphoreType.DMA((total,))],
        compiler_params=pltpu.CompilerParams(vmem_limit_bytes=16 << 20),
        cost_estimate=pl.CostEstimate(flops=0, transcendentals=0, bytes_accessed=4 * total * item_bytes),
        name="pick_items",
    )(table, own, *arrays)


class Order:
    def __init__(self):
        self.last = ()

    def add(self, *values):
        self.last = values

    def follow(self, value):
        return after(value, *self.last) if self.last else value


def exchange(pieces, axes):
    return lax.all_to_all(pieces, axes, split_axis=0, concat_axis=0, tiled=True)


def spread(own, doc_of, levels):
    lanes, blocks, part, width = own.shape
    pieces = jnp.moveaxis(own.reshape(lanes, blocks, levels, part // levels, width), 2, 0)
    dealt = exchange(pieces, "z").reshape(levels * lanes, blocks, part // levels, width)
    placed = jnp.take(dealt, doc_of, axis=0).reshape(pieces.shape)
    return jnp.moveaxis(exchange(placed, "z"), 0, 2).reshape(own.shape)


class Route:
    def __init__(self, own, table, problem, origin, steps, horizon, levels):
        self.own, self.table, self.problem, self.origin = own, table, problem, origin
        self.steps, self.horizon, self.levels = steps, horizon, levels
        self.rights, self.lefts = [], []

    def step(self, order):
        self.rights, self.lefts = self.stepped(self.rights, self.lefts, self.own, self.table, order)

    def stepped(self, rights, lefts, own, table, order=None):
        ways = (0, [(i, i + 1) for i in range(self.levels - 1)]), (self.horizon, [(i + 1, i) for i in range(self.levels - 1)])
        came = []
        for arrivals, (first, pairs) in zip((rights, lefts), ways):
            lanes, count = own.shape[0], len(arrivals)
            allowed = [(index, index) for index in range(lanes + count)]
            entries = order.follow(table) if order else table
            (outgoing,) = pick(entries, self.problem, own, arrivals, ((0, first + count, allowed),))
            if order:
                order.add(outgoing)
            came.append(arrivals + [lax.ppermute(outgoing, "z", pairs)])
        return came

    def settle(self, rights, lefts, own, table):
        lanes, count = own.shape[0], len(rights)
        allowed = [(lane, lane) for lane in range(lanes)]
        allowed += [(lanes + t, lanes + t) for t in range(count)]
        allowed += [(lanes + self.horizon + t, lanes + count + t) for t in range(count)]
        return pick(table, self.problem, own, rights + lefts, ((lanes, 2 * self.horizon, allowed),))[0]

    def finish(self, rights, lefts, own, table):
        lanes = own.shape[0]

        def more(rights, lefts, own, table):
            if len(rights) == self.horizon:
                everything = lax.all_gather(own, "z", axis=0, tiled=True)
                return jnp.take(everything, self.origin, axis=0)
            rights, lefts = self.stepped(rights, lefts, own, table)
            return self.finish(rights, lefts, own, table)

        needed = table[self.problem, 2 * self.horizon + lanes]
        return lax.cond(needed > len(rights), more, self.settle, rights, lefts, own, table)

    def result(self, *earlier):
        table = after(self.table, *earlier) if earlier else self.table
        return self.finish(self.rights, self.lefts, self.own, table)


def pack_kernel(*refs):
    out_ref = refs[-1]
    for number, ref in enumerate(refs[:-1]):
        out_ref[:, number] = ref[0, 0].reshape(out_ref.shape[0], *out_ref.shape[2:])


def pack(section, lanes, blocks):
    block_rows, width = blocks[0].shape[2:]
    part = block_rows // lanes
    shape = (lanes, len(blocks), part, width)
    each = math.gcd(2, lanes)
    return pl.pallas_call(
        pack_kernel,
        grid=(lanes // each,),
        in_specs=[pl.BlockSpec((1, 1, each * part, width), lambda lane: (section, 0, lane, 0)) for _ in blocks],
        out_specs=pl.BlockSpec((each,) + shape[1:], lambda lane: (lane, 0, 0, 0)),
        out_shape=jax.ShapeDtypeStruct(shape, blocks[0].dtype),
        cost_estimate=pl.CostEstimate(flops=0, transcendentals=0, bytes_accessed=4 * math.prod(shape)),
        name="pack_blocks",
    )(*blocks)


def after(value, *others):
    return lax.optimization_barrier((value,) + others)[0]


def body(state, keys, values, queries, rates, remaining, first_owner, migration):
    levels = lax.axis_size("z")
    lanes = lax.axis_size(LEVEL)
    devices = levels * lanes
    myself = lax.axis_index(GROUP)
    my_level = lax.axis_index("z")
    block_rows, width = keys.shape[2], keys.shape[3]
    piece_rows = block_rows // devices
    packed_first = pack(0, lanes, (keys, values, queries))
    own_first = exchange(packed_first, LEVEL)

    doc_first = inverse_of(first_owner)
    doc_here = doc_first[myself]
    steps = (devices // 4 + 1, devices // 8 + 1)
    horizon = steps[0] + EXTRA
    has_second = (remaining >= 2).astype(jnp.int32)
    rates_here = lax.dynamic_index_in_dim(rates, doc_here, 1, keepdims=False)
    source_of = inverse_of(migration)
    blocks = (keys, values, queries)

    if horizon > LONGEST:
        own_second = exchange(pack(1, lanes, blocks), LEVEL)
        blocks_first = exchange(spread(own_first, doc_first, levels), LEVEL)
        blocks_second = exchange(spread(own_second, doc_first, levels), LEVEL)
    else:
        origin = lax.dynamic_slice_in_dim(doc_first, my_level * lanes, lanes, 0)
        targets = jnp.stack([first_owner, first_owner])
        live = jnp.stack([jnp.ones_like(has_second), has_second])
        table = plan_routes(levels, lanes, horizon, my_level, targets, live)
        first = Route(own_first, table, 0, origin, steps[0], horizon, levels)
        order = Order()
        first.step(order)
        own_second = exchange(order.follow(after(pack(1, lanes, blocks), table)), LEVEL)
        second = Route(own_second, table, 1, origin, steps[1], horizon, levels)
        for step in range(1, max(steps[0], steps[1] + LAG)):
            if step >= LAG and step - LAG < steps[1]:
                second.step(order)
            if step < steps[0]:
                first.step(order)
        blocks_first = exchange(first.result(second.rights[-1], second.lefts[-1]), LEVEL)
        blocks_second = exchange(second.result(), LEVEL)

    always = jnp.ones((), jnp.int32)
    result_one, updated = run_document(always, blocks_first, rates_here[0], state, True)
    dealt_one = exchange(result_one.reshape(devices, piece_rows, width), GROUP)
    (result_two,) = run_document(has_second[doc_here], blocks_second, rates_here[1], updated, False)
    both = jnp.stack([jnp.take(dealt_one, first_owner, axis=0), result_two.reshape(devices, piece_rows, width)], axis=1)
    both = exchange(both, GROUP)
    round_one, dealt_two = both[:, 0], both[:, 1]
    round_two = exchange(jnp.take(dealt_two, source_of, axis=0), GROUP)
    return round_one.reshape(1, block_rows, width), round_two.reshape(1, block_rows, width)


def solution(mesh):
    groups, along, cores = (mesh.shape[name] for name in ("grp", "seq", "doc"))
    wide = max(d for d in range(1, along + 1) if along % d == 0 and d**3 <= along)
    fine = Mesh(mesh.devices.reshape(groups, along // wide, wide, cores), ("grp",) + GROUP)
    everywhere = ("grp",) + GROUP
    return jax.shard_map(
        body,
        mesh=fine,
        in_specs=(
            P(everywhere, None, None, None),
            P(None, everywhere, None, None),
            P(None, everywhere, None, None),
            P(None, everywhere, None, None),
            P(None, "grp", None),
            P("grp"),
            P("grp"),
            P("grp"),
        ),
        out_specs=(P(everywhere, None, None), P(everywhere, None, None)),
        check_vma=False,
    )
```
